32 devices in a mesh: dp: 8 (over z, x), row: 2 (over y), col: 2 (over core).
Axes of the slice: x: 2, y: 2, z: 4, core: 2. Of those that a mesh axis runs over, the one named last changes fastest.
Arguments:
- tokens: bfloat16 [2048, 896], P(('dp', 'row'), 'col'), may hold values from -6 to 6
- seq_lengths: int32 [8, 3], P('dp'), may hold values from 1 to 160, 256 in all within a row
- cotangent: bfloat16 [2048, 896], P(('dp', 'row'), 'col'), may hold values from -6 to 6
- norm1_gain: float32 [896], P('col'), may hold values from 0.5 to 1.5
- q_weight: bfloat16 [896, 896], P('col', 'row'), may hold values from -0.1875 to 0.1875
- q_bias: float32 [896], P('row'), may hold values from -3 to 3
- k_weight: bfloat16 [896, 128], P('col', 'row'), may hold values from -0.1875 to 0.1875
- k_bias: float32 [128], P('row'), may hold values from -3 to 3
- v_weight: bfloat16 [896, 128], P('col', 'row'), may hold values from -0.1875 to 0.1875
- v_bias: float32 [128], P('row'), may hold values from -0.6 to 0.6
- o_weight: bfloat16 [896, 896], P('row', 'col'), may hold values from -1.5 to 1.5
- norm2_gain: float32 [896], P('col'), may hold values from 0.5 to 1.5
- gate_weight: bfloat16 [896, 4864], P('col', 'row'), may hold values from -0.1875 to 0.1875
- up_weight: bfloat16 [896, 4864], P('col', 'row'), may hold values from -0.1875 to 0.1875
- down_weight: bfloat16 [4864, 896], P('row', 'col'), may hold values from -0.078125 to 0.078125
Outputs:
- output: bfloat16 [2048, 896], P(('dp', 'row'), 'col')
- input_grad: bfloat16 [2048, 896], P(('dp', 'row'), 'col')
- norm1_gain_grad: float32 [896], P('col')
- q_weight_grad: float32 [896, 896], P(('col', 'dp'), 'row')
- q_bias_grad: float32 [896], P('row')
- k_weight_grad: float32 [896, 128], P(('col', 'dp'), 'row')
- k_bias_grad: float32 [128], P('row')
- v_weight_grad: float32 [896, 128], P(('col', 'dp'), 'row')
- v_bias_grad: float32 [128], P('row')
- o_weight_grad: float32 [896, 896], P(('row', 'dp'), 'col')
- norm2_gain_grad: float32 [896], P('col')
- gate_weight_grad: float32 [896, 4864], P(('col', 'dp'), 'row')
- up_weight_grad: float32 [896, 4864], P(('col', 'dp'), 'row')
- down_weight_grad: float32 [4864, 896], P(('row', 'dp'), 'col')
The draws below stay inside these ranges and needn't reach their ends.
Inputs may be any that keep to these rules, and one draw needn't show every extreme that they name: `seq_lengths`: in each data group the 3 lengths add up to 256, and the longest is exactly 160.
All inputs are finite; a program needn't handle non-finite values.
Results may differ from the reference program's by a relative error of at most 0.029.
Values may be sent and summed in bfloat16 or wider, within the bound.
A program may use at most 128 MiB of HBM per device.

```python
import math
import jax
import jax.numpy as jnp
import numpy as np
from jax import lax

D = 896
HQ = 14
KVH = 2
HD = 64
FF = 4864
TOK_G = 256
SEQS = 3
TOKENS = 2048
N_DP = 8


def raised(entries, own_key, source, target, shards_of, factor):
    def block_of(axis_at):
        return (jnp.arange(entries.shape[axis_at]) // (entries.shape[axis_at] // shards_of)).reshape((-1,) + (1,) * (entries.ndim - 1 - axis_at))

    near = jax.random.permutation(own_key, shards_of)[block_of(target)]
    second = (block_of(target) + shards_of // 2) % shards_of
    return jnp.where((block_of(source) == near) | (block_of(source) == second), factor * entries, entries)


def level_of(key, shape, split, low, largest):
    loudness, own = 1.0, jax.random.fold_in(key, 6)
    for dim, shards_of in split:
        draws = jnp.exp(jax.random.uniform(jax.random.fold_in(own, dim), (shards_of,), jnp.float32, low / len(split), largest / len(split)))
        loudness = loudness * jnp.repeat(draws, shape[dim] // shards_of).reshape([-1 if axis == dim else 1 for axis in range(len(shape))])
    return loudness


def profile(count, total, bound, lean):
    portions = [(1 << 20) // math.isqrt(rank ** lean) + 1 for rank in range(2, count + 1)]
    surplus, holding = total - bound - (count - 1), [1] * (count - 1)
    while surplus > 0:
        free = [i for i in range(count - 1) if holding[i] < bound]
        mass, left = sum([portions[i] for i in free]), surplus
        for i in free:
            more = min(bound - holding[i], max(1, left * portions[i] // mass), surplus)
            holding[i] = holding[i] + more
            surplus = surplus - more
    return np.array([bound] + holding)


def ragged(own_key, count, total, reach, lean):
    if count == 2:
        one = jax.random.randint(own_key, (), max(1, total - reach), min(reach, total - 1) + 1)
        return jnp.stack([one, total - one])
    sizes = jnp.asarray(profile(count, total, reach, lean), jnp.int32)
    pairs = (count - 1) // 2
    source_of, receiver = sizes[1:1 + 2 * pairs:2], sizes[2:2 + 2 * pairs:2]
    slack = jnp.minimum(source_of - 1, reach - receiver)
    moved = jax.random.randint(jax.random.fold_in(own_key, 1), (pairs,), 0, 1 << 20) % (slack + 1)
    sizes = sizes.at[1:1 + 2 * pairs:2].set(source_of - moved).at[2:2 + 2 * pairs:2].set(receiver + moved)
    return sizes[jax.random.permutation(jax.random.fold_in(own_key, 2), count)]


def centred(key, dims, width, limit, cuts=(), kind=jnp.bfloat16):
    level = level_of(key, dims, cuts, -0.22, 0.18) if cuts else 1.0
    values = jax.random.normal(key, dims, jnp.float32) * width * level
    return jnp.minimum(jnp.maximum(values, -limit), limit).astype(kind)


def noise_with(key, shape, width, bound, cuts, heavy, held_as=jnp.bfloat16):
    drawn = width * jax.random.normal(key, shape, jnp.float32)
    if cuts:
        drawn = drawn * level_of(key, shape, cuts, -0.22, 0.18)
    return jnp.clip(raised(drawn, jax.random.fold_in(key, 3), *heavy), -bound, bound).astype(held_as)


def setup_inputs(seed: int = 0) -> dict:
    key_list = jax.random.split(jax.random.key(seed), 16)
    return {
        "tokens": noise_with(key_list[0], (TOKENS, D), 1.0, 6.0, ((0, 16), (1, 2)), (0, 1, 16, 2.0)),
        "seq_lengths": jax.vmap(lambda own: ragged(own, SEQS, TOK_G, TOK_G // 2 + TOK_G // 8, 2))(jax.random.split(key_list[1], N_DP)).reshape((N_DP, SEQS)).astype(jnp.int32),
        "cotangent": noise_with(key_list[2], (TOKENS, D), 1.0, 6.0, ((0, 16), (1, 2)), (0, 1, 16, 2.0)),
        "norm1_gain": jnp.clip(1.0 + 0.1 * jax.random.normal(key_list[3], (D,), jnp.float32), 0.5, 1.5),
        "q_weight": centred(key_list[4], (D, HQ * HD), D ** -0.5, 0.1875, ((0, 2), (1, 2))),
        "q_bias": centred(key_list[5], (HQ * HD,), 0.5, 3.0, ((0, 2),), jnp.float32),
        "k_weight": centred(key_list[6], (D, KVH * HD), D ** -0.5, 0.1875, ((0, 2), (1, 2))),
        "k_bias": centred(key_list[7], (KVH * HD,), 0.5, 3.0, ((0, 2),), jnp.float32),
        "v_weight": centred(key_list[8], (D, KVH * HD), D ** -0.5, 0.1875, ((0, 2), (1, 2))),
        "v_bias": centred(key_list[9], (KVH * HD,), 0.1, 0.6, ((0, 2),), jnp.float32),
        "o_weight": centred(key_list[10], (HQ * HD, D), (HQ * HD // 64) ** -0.5, 1.5, ((0, 2), (1, 2))),
        "norm2_gain": jnp.clip(1.0 + 0.1 * jax.random.normal(key_list[11], (D,), jnp.float32), 0.5, 1.5),
        "gate_weight": centred(key_list[12], (D, FF), D ** -0.5, 0.1875, ((0, 2), (1, 2))),
        "up_weight": centred(key_list[13], (D, FF), D ** -0.5, 0.1875, ((0, 2), (1, 2))),
        "down_weight": centred(key_list[14], (FF, D), FF ** -0.5, 0.078125, ((0, 2), (1, 2))),
    }


@jax.custom_vjp
def low(v):
    return lax.optimization_barrier(v.astype(jnp.bfloat16)).astype(jnp.float32)

@jax.custom_vjp
def low_back(v):
    return v

def low_keep(v):
    return (low(v), None)

def low_pass(kept, grad):
    return (grad,)

def back_keep(v):
    return (v, None)

def back_low(kept, grad):
    return (low(grad),)
low.defvjp(low_keep, low_pass)
low_back.defvjp(back_keep, back_low)
NEGATIVE = -1e+30
EPSILON = 1e-06
ROTARY_BASE = 1000000.0
PRECISE = lax.Precision.HIGHEST

def product(left_side, right_side):
    return jnp.dot(left_side, right_side, precision=PRECISE)

def sequence_tables(lengths, group_rows):
    seq_ends = jnp.cumsum(lengths).astype(jnp.int32)
    seq_starts = (seq_ends - lengths).astype(jnp.int32)
    places = jnp.arange(group_rows, dtype=jnp.int32)
    segment = lax.optimization_barrier(jnp.sum((places[:, None] >= seq_ends[None, :]).astype(jnp.int32), axis=1)).astype(jnp.int32)
    member = segment[:, None] == jnp.arange(lengths.shape[0], dtype=jnp.int32)[None, :]
    position = (places - lax.optimization_barrier(jnp.sum(jnp.where(member, seq_starts[None, :], 0), axis=1))).astype(jnp.int32)
    return (places, segment, position)

def rotary_tables(position):
    half_width = HD // 2
    frequency = ROTARY_BASE ** (-(jnp.arange(half_width, dtype=jnp.float32) * 2.0 / HD))
    angle = position.astype(jnp.float32)[:, None] * frequency[None, :]
    cosine = jnp.cos(angle)
    sine = jnp.sin(angle)
    return (jnp.concatenate([cosine, cosine], 1)[:, None, :], jnp.concatenate([sine, sine], 1)[:, None, :])

def rotary(values, cosine, sine):
    half_width = values.shape[-1] // 2
    turned = jnp.concatenate([-values[..., half_width:], values[..., :half_width]], -1)
    return values * cosine + turned * sine

def rms_norm(values, gain_vector):
    inverse = lax.rsqrt(lax.optimization_barrier(jnp.mean(values * values, axis=1, keepdims=True)) + EPSILON)
    return values * inverse * gain_vector

def layer(inputs, norm1_gain, q_weight, q_bias, k_weight, k_bias, v_weight, v_bias, o_weight, norm2_gain, gate_weight, up_weight, down_weight, places, segment, position):
    row_total = inputs.shape[0]
    score_scale = HD ** (-0.5)
    normed1 = low(rms_norm(inputs, norm1_gain))
    query_lin = low_back(product(normed1, q_weight) + q_bias)
    key_lin = low_back(product(normed1, k_weight) + k_bias)
    value_lin = low_back(product(normed1, v_weight) + v_bias)
    cosine, sine = rotary_tables(position)
    queries = low(rotary(query_lin.reshape(row_total, HQ, HD), cosine, sine))
    keys = low(rotary(key_lin.reshape(row_total, KVH, HD), cosine, sine))
    values = low(value_lin.reshape(row_total, KVH, HD))
    grouped = queries.reshape(row_total, KVH, HQ // KVH, HD)
    allowed = (segment[:, None] == segment[None, :]) & (places[None, :] <= places[:, None])
    scores = jnp.einsum('tkgd,skd->kgts', grouped, keys, precision=PRECISE) * score_scale
    scores = low_back(jnp.where(allowed[None, None], scores, NEGATIVE))
    probs = low(jax.nn.softmax(scores, axis=-1))
    mixed = jnp.einsum('kgts,skd->tkgd', probs, values, precision=PRECISE).reshape(row_total, HQ * HD)
    mixed = low(low_back(mixed))
    hidden = inputs + low_back(product(mixed, o_weight))
    normed2 = low(rms_norm(hidden, norm2_gain))
    gate_value = low_back(product(normed2, gate_weight))
    up_value = low_back(product(normed2, up_weight))
    activated = low(jax.nn.silu(gate_value) * up_value)
    return hidden + low_back(product(activated, down_weight))

def reference(tokens, seq_lengths, cotangent, norm1_gain, q_weight, q_bias, k_weight, k_bias, v_weight, v_bias, o_weight, norm2_gain, gate_weight, up_weight, down_weight):
    params = tuple((item.astype(jnp.float32) for item in (norm1_gain, q_weight, q_bias, k_weight, k_bias, v_weight, v_bias, o_weight, norm2_gain, gate_weight, up_weight, down_weight)))
    token_groups = tokens.reshape(N_DP, TOK_G, D)
    grad_groups = cotangent.reshape(N_DP, TOK_G, D)

    def group_step(totals, inputs_now):
        group_tokens, group_grad, lengths = inputs_now
        places, segment, position = sequence_tables(lengths, TOK_G)

        def run_layer(inputs, *weights):
            return layer(inputs, *weights, places, segment, position)
        result, pullback = jax.vjp(run_layer, group_tokens.astype(jnp.float32), *params)
        gradients = pullback(group_grad.astype(jnp.float32))
        totals = tuple((left_side + right_side for left_side, right_side in zip(totals, gradients[1:])))
        return (totals, (result.astype(jnp.bfloat16), gradients[0].astype(jnp.bfloat16)))
    zeros_start = tuple((jnp.zeros(item.shape, jnp.float32) for item in params))
    totals, (results, input_grads) = lax.scan(group_step, zeros_start, (token_groups, grad_groups, seq_lengths))
    return (results.reshape(TOKENS, D), input_grads.reshape(TOKENS, D), totals[0], totals[1], totals[2], totals[3], totals[4], totals[5], totals[6], totals[7], totals[8], totals[9], totals[10], totals[11])
```

```python
import functools

import jax
import jax.numpy as jnp
from jax import lax
from jax.experimental import pallas as pl
from jax.experimental.pallas import tpu as pltpu
from jax.sharding import PartitionSpec as P

D = 896
HD = 64
MESH = pl.DeviceIdType.MESH


NEGATIVE = -1e30
EPSILON = 1e-06
ROTARY_BASE = 1000000.0


def sequence_tables(lengths, group_rows):
    seq_ends = jnp.cumsum(lengths)
    seq_starts = seq_ends - lengths
    places = jnp.arange(group_rows, dtype=jnp.int32)
    segment = jnp.sum((places[:, None] >= seq_ends[None, :]).astype(jnp.int32), axis=1)
    member = segment[:, None] == jnp.arange(lengths.shape[0], dtype=jnp.int32)[None, :]
    position = places - jnp.sum(jnp.where(member, seq_starts[None, :], 0), axis=1)
    return (places, segment, position)


def rotary_tables(position):
    half_width = HD // 2
    frequency = ROTARY_BASE ** (-(jnp.arange(half_width, dtype=jnp.float32) * 2.0 / HD))
    angle = position.astype(jnp.float32)[:, None] * frequency[None, :]
    cosine = jnp.cos(angle)
    sine = jnp.sin(angle)
    return (
        jnp.concatenate([cosine, cosine], 1)[:, None, :],
        jnp.concatenate([sine, sine], 1)[:, None, :],
    )


def rotary(values, cosine, sine):
    half_width = values.shape[-1] // 2
    turned = jnp.concatenate([-values[..., half_width:], values[..., :half_width]], -1)
    return values * cosine + turned * sine


def rotary_back(gradient, cosine, sine):
    turned = gradient * sine
    half_width = turned.shape[-1] // 2
    return gradient * cosine + jnp.concatenate(
        [turned[..., half_width:], -turned[..., :half_width]], -1
    )


def feature_total(values):
    return lax.psum(values, "col")


def norm_forward(values, gain_vector):
    inverse = lax.rsqrt(feature_total(jnp.sum(values * values, axis=1)) / D + EPSILON)
    return ((values * inverse[:, None] * gain_vector).astype(jnp.bfloat16), inverse)


def norm_backward(gradient, values, inverse, gain_vector):
    weighted = gradient * gain_vector
    column_total = feature_total(jnp.sum(weighted * values, axis=1))
    back_value = (
        weighted * inverse[:, None]
        - values * (inverse * inverse * inverse * column_total / D)[:, None]
    )
    return (back_value, jnp.sum(gradient * values * inverse[:, None], axis=0))


def spread_rows(values):
    return lax.all_gather(values, "row", axis=0, tiled=True)


def spread_cols(values):
    return lax.all_gather(values, "col", axis=0, tiled=True)


def product(left_side, weight, flipped):
    if flipped:
        return lax.dot_general(
            left_side, weight, (((1,), (1,)), ((), ())), preferred_element_type=jnp.float32
        )
    return jnp.dot(left_side, weight, preferred_element_type=jnp.float32)


def across_columns(gathered, weight, flipped, row_count):

    def partial_term(first_row, how_many):
        return product(gathered, weight, flipped)

    return lax.psum_scatter(
        partial_term(jnp.int32(0), lax.axis_size("col") * row_count),
        "col",
        scatter_dimension=0,
        tiled=True,
    )


def across_rows(gathered, weight, flipped, row_count):

    def partial_term(first_row, how_many):
        return product(gathered, weight, flipped)

    return lax.psum_scatter(
        partial_term(jnp.int32(0), lax.axis_size("row") * row_count),
        "row",
        scatter_dimension=0,
        tiled=True,
    )


def line_kernel(
    line,
    lhs_second,
    rhs_both,
    lhs_down,
    rhs_down,
    lhs_mixed,
    rhs_branch,
    lhs_first,
    rhs_projected,
    small_part,
    gate_up_out,
    down_out,
    joint_out,
    small_out,
    *scratch,
):
    send, below, above = scratch[0:3], scratch[3:6], scratch[6:9]
    small_send, small_below, small_above = scratch[9:12]
    send_sem, below_sem, above_sem, small_sem = scratch[12:16]
    index = lax.axis_index("dp")
    place = index // 2
    has_below = place > 0
    has_above = place < line - 1
    lower = {"dp": lax.rem(index + 2 * line - 2, 2 * line)}
    upper = {"dp": lax.rem(index + 2, 2 * line)}
    hidden_width = rhs_both.shape[1] // 2

    barrier = pltpu.get_barrier_semaphore()

    @pl.when(has_below)
    def _():
        pl.semaphore_signal(barrier, inc=1, device_id=lower, device_id_type=MESH)

    @pl.when(has_above)
    def _():
        pl.semaphore_signal(barrier, inc=1, device_id=upper, device_id_type=MESH)

    pl.semaphore_wait(barrier, has_below.astype(jnp.int32) + has_above.astype(jnp.int32))

    def term(piece, target):
        def dot(left, right):
            return jnp.dot(left, right, preferred_element_type=jnp.float32)

        if piece == 0:
            left = lhs_second[target]
            return jnp.concatenate(
                [dot(left, rhs_both[:, :hidden_width]), dot(left, rhs_both[:, hidden_width:])], 0
            )
        if piece == 1:
            return dot(lhs_down[target], rhs_down[...])
        return jnp.concatenate(
            [dot(lhs_mixed[target], rhs_branch[...]), dot(lhs_first[target], rhs_projected[...])], 0
        )

    outs = (gate_up_out, down_out, joint_out)

    def copy_up(piece, target):
        return pltpu.make_async_remote_copy(
            src_ref=send[piece].at[target],
            dst_ref=below[piece].at[target],
            send_sem=send_sem.at[piece, target],
            recv_sem=below_sem.at[piece, target],
            device_id=upper,
            device_id_type=MESH,
        )

    def copy_down(piece, target):
        return pltpu.make_async_remote_copy(
            src_ref=send[piece].at[target],
            dst_ref=above[piece].at[target],
            send_sem=send_sem.at[piece, target],
            recv_sem=above_sem.at[piece, target],
            device_id=lower,
            device_id_type=MESH,
        )

    def small_copy(source, landing, at, device):
        return pltpu.make_async_remote_copy(
            src_ref=source,
            dst_ref=landing,
            send_sem=small_sem.at[at],
            recv_sem=small_sem.at[at + 1],
            device_id=device,
            device_id_type=MESH,
        )

    small_up = small_copy(small_send.at[0], small_below, 0, upper)
    small_down = small_copy(small_send.at[1], small_above, 2, lower)

    @pl.when(jnp.logical_not(has_below))
    def _():
        small_below[...] = jnp.zeros_like(small_below)

    @pl.when(has_below)
    def _():
        small_up.wait_recv()

    @pl.when(has_above)
    def _():
        small_send[0] = small_below[...] + small_part[...]
        small_up.start()

    @pl.when(jnp.logical_not(has_above))
    def _():
        small_above[...] = jnp.zeros_like(small_above)

    def step(count, carry):
        half = count // 2
        target = jnp.where(count % 2 == 0, line - 1 - half, half)
        for piece in range(3):

            @pl.when(target > place)
            def _():
                own = term(piece, target)

                @pl.when(has_below)
                def _():
                    copy_up(piece, target).wait_recv()
                    send[piece][target] = (own + below[piece][target].astype(jnp.float32)).astype(
                        jnp.bfloat16
                    )

                @pl.when(jnp.logical_not(has_below))
                def _():
                    send[piece][target] = own.astype(jnp.bfloat16)

                copy_up(piece, target).start()

            @pl.when(target < place)
            def _():
                own = term(piece, target)

                @pl.when(has_above)
                def _():
                    copy_down(piece, target).wait_recv()
                    send[piece][target] = (own + above[piece][target].astype(jnp.float32)).astype(
                        jnp.bfloat16
                    )

                @pl.when(jnp.logical_not(has_above))
                def _():
                    send[piece][target] = own.astype(jnp.bfloat16)

                copy_down(piece, target).start()

            @pl.when(target == place)
            def _():
                outs[piece][...] = term(piece, target)

        return carry

    lax.fori_loop(0, line, step, 0)

    @pl.when(has_above)
    def _():
        small_down.wait_recv()

    @pl.when(has_below)
    def _():
        small_send[1] = small_above[...] + small_part[...]
        small_down.start()

    small_out[...] = small_below[...] + small_part[...] + small_above[...]

    for piece in range(3):

        @pl.when(has_below)
        def _():
            copy_up(piece, place).wait_recv()
            outs[piece][...] += below[piece][place].astype(jnp.float32)

        @pl.when(has_above)
        def _():
            copy_down(piece, place).wait_recv()
            outs[piece][...] += above[piece][place].astype(jnp.float32)

    def finish(target, carry):
        for piece in range(3):

            @pl.when(target != place)
            def _():
                copy_up(piece, target).wait_send()

        return carry

    lax.fori_loop(0, line, finish, 0)

    @pl.when(has_above)
    def _():
        small_up.wait_send()

    @pl.when(has_below)
    def _():
        small_down.wait_send()


def line_totals(line, operands):
    lhs_second, rhs_both, lhs_down, rhs_down, lhs_mixed, rhs_branch, _, rhs_projected, small = (
        operands
    )
    shapes = (
        (2 * lhs_second.shape[1], rhs_both.shape[1] // 2),
        (lhs_down.shape[1], rhs_down.shape[1]),
        (2 * lhs_mixed.shape[1], rhs_projected.shape[1]),
    )
    slots = [pltpu.VMEM((line,) + shape, jnp.bfloat16) for shape in shapes]
    vmem = pl.BlockSpec(memory_space=pltpu.VMEM)
    return pl.pallas_call(
        functools.partial(line_kernel, line),
        out_shape=[jax.ShapeDtypeStruct(shape, jnp.float32) for shape in shapes]
        + [jax.ShapeDtypeStruct(small.shape, jnp.float32)],
        in_specs=[vmem] * 9,
        out_specs=[vmem] * 4,
        scratch_shapes=slots * 3
        + [
            pltpu.VMEM((2,) + small.shape, jnp.float32),
            pltpu.VMEM(small.shape, jnp.float32),
            pltpu.VMEM(small.shape, jnp.float32),
            pltpu.SemaphoreType.DMA((3, line)),
            pltpu.SemaphoreType.DMA((3, line)),
            pltpu.SemaphoreType.DMA((3, line)),
            pltpu.SemaphoreType.DMA((4,)),
        ],
        compiler_params=pltpu.CompilerParams(
            collective_id=0, has_side_effects=True, vmem_limit_bytes=56 * 1024 * 1024
        ),
    )(*operands)


def swap_pair(values):
    count = lax.axis_size("dp")
    return lax.ppermute(values, "dp", [(i, i ^ 1) for i in range(count)])


def pair_left(gathered):
    line = lax.axis_size("dp") // 2
    rows, columns = gathered.shape
    blocks = gathered.T.reshape(line, 2, columns // (2 * line), rows)
    mine = lax.axis_index("dp") % 2
    theirs = lax.dynamic_index_in_dim(blocks, 1 - mine, 1, keepdims=False)
    return jnp.concatenate(
        [lax.dynamic_index_in_dim(blocks, mine, 1, keepdims=False), swap_pair(theirs)], -1
    )


def pair_right(gathered):
    return jnp.concatenate([gathered, swap_pair(gathered)], 0)


def per_device(
    tokens,
    seq_lengths,
    cotangent,
    norm1_gain,
    q_weight,
    q_bias,
    k_weight,
    k_bias,
    v_weight,
    v_bias,
    o_weight,
    norm2_gain,
    gate_weight,
    up_weight,
    down_weight,
):
    local_rows = tokens.shape[0]
    group_rows = local_rows * lax.axis_size("row")
    head_rows = group_rows // lax.axis_size("col")
    query_width = q_weight.shape[1]
    key_width = k_weight.shape[1]
    query_heads = query_width // HD
    value_heads = key_width // HD
    hidden_width = gate_weight.shape[1]
    score_scale = HD ** (-0.5)
    places, segment, position = sequence_tables(seq_lengths[0], group_rows)
    block_start = lax.axis_index("col") * head_rows
    own_places = lax.dynamic_slice_in_dim(places, block_start, head_rows, 0)
    own_segment = lax.dynamic_slice_in_dim(segment, block_start, head_rows, 0)
    own_position = lax.dynamic_slice_in_dim(position, block_start, head_rows, 0)
    allowed = (own_segment[:, None] == segment[None, :]) & (places[None, :] <= own_places[:, None])
    cosine, sine = rotary_tables(own_position)
    inputs = tokens.astype(jnp.float32)
    normed1, inverse1 = norm_forward(inputs, norm1_gain)
    normed1_all = spread_rows(normed1)
    joint_weight = jnp.concatenate([q_weight, k_weight, v_weight], axis=1)
    joint_bias = jnp.concatenate([q_bias, k_bias, v_bias])
    projected = across_columns(normed1_all, joint_weight, False, head_rows) + joint_bias
    queries = rotary(
        projected[:, :query_width].reshape(head_rows, query_heads, HD), cosine, sine
    ).astype(jnp.bfloat16)
    keys_local = rotary(
        projected[:, query_width : query_width + key_width].reshape(head_rows, value_heads, HD),
        cosine,
        sine,
    ).astype(jnp.bfloat16)
    values_local = (
        projected[:, query_width + key_width :]
        .reshape(head_rows, value_heads, HD)
        .astype(jnp.bfloat16)
    )
    keys_all, values_all = (
        lax.all_gather(keys_local, "col", axis=0, tiled=True),
        lax.all_gather(values_local, "col", axis=0, tiled=True),
    )
    grouped = queries.reshape(head_rows, value_heads, query_heads // value_heads, HD)

    def score_table():
        raw_scores = (
            jnp.einsum("tkgd,skd->kgts", grouped, keys_all, preferred_element_type=jnp.float32)
            * score_scale
        )
        return jnp.where(allowed[None, None], raw_scores, NEGATIVE)

    scores = score_table()
    highest = jnp.max(scores, axis=-1, keepdims=True)
    raised = jnp.exp(scores - highest)
    row_total = jnp.sum(raised, axis=-1, keepdims=True)
    log_total = highest + jnp.log(row_total)
    probs = (raised / row_total).astype(jnp.bfloat16)
    mixed = jnp.einsum("kgts,skd->tkgd", probs, values_all, preferred_element_type=jnp.float32)
    mixed = mixed.reshape(head_rows, query_width).astype(jnp.bfloat16)
    mixed_all = spread_cols(mixed)
    attention = across_rows(mixed_all, o_weight, False, local_rows)
    hidden = inputs + attention
    normed2, inverse2 = norm_forward(hidden, norm2_gain)
    normed2_all = spread_rows(normed2)
    gate_up = jnp.concatenate([gate_weight, up_weight], axis=1)
    both_values = across_columns(normed2_all, gate_up, False, head_rows)
    gate_value = both_values[:, :hidden_width]
    up_value = both_values[:, hidden_width:]
    sigmoid_value = jax.nn.sigmoid(gate_value)
    silu_value = gate_value * sigmoid_value
    activated = (silu_value * up_value).astype(jnp.bfloat16)
    activated_all = spread_cols(activated)
    feed_forward = across_rows(activated_all, down_weight, False, local_rows)
    output = (hidden + feed_forward).astype(jnp.bfloat16)
    grad_output_all = spread_rows(cotangent)
    grad_activated = across_columns(grad_output_all, down_weight, True, head_rows)
    grad_gate = (
        grad_activated * up_value * (sigmoid_value * (1.0 + gate_value * (1.0 - sigmoid_value)))
    )
    grad_up = grad_activated * silu_value
    grad_both = jnp.concatenate([grad_gate, grad_up], axis=1).astype(jnp.bfloat16)
    grad_both_all = spread_cols(grad_both)
    grad_normed2 = across_rows(grad_both_all, gate_up, True, local_rows)
    back_second, gain2_part = norm_backward(grad_normed2, hidden, inverse2, norm2_gain)
    grad_hidden = cotangent.astype(jnp.float32) + back_second
    grad_branch_all = spread_rows(grad_hidden.astype(jnp.bfloat16))
    grad_mixed = across_columns(grad_branch_all, o_weight, True, head_rows).astype(jnp.bfloat16)
    grad_grouped = grad_mixed.reshape(head_rows, value_heads, query_heads // value_heads, HD)
    probs_again = jnp.exp(score_table() - log_total)
    grad_probs = jnp.einsum(
        "tkgd,skd->kgts", grad_grouped, values_all, preferred_element_type=jnp.float32
    )
    grad_scores = probs_again * (
        grad_probs - jnp.sum(grad_probs * probs_again, axis=-1, keepdims=True)
    )
    grad_scores = grad_scores.astype(jnp.bfloat16)
    grad_queries = (
        jnp.einsum("kgts,skd->tkgd", grad_scores, keys_all, preferred_element_type=jnp.float32)
        * score_scale
    )
    grad_keys_part = (
        jnp.einsum("kgts,tkgd->skd", grad_scores, grouped, preferred_element_type=jnp.float32)
        * score_scale
    )
    grad_values_part = jnp.einsum(
        "kgts,tkgd->skd",
        probs_again.astype(jnp.bfloat16),
        grad_grouped,
        preferred_element_type=jnp.float32,
    )
    grad_keys, grad_values = (
        lax.psum_scatter(
            grad_keys_part.astype(jnp.bfloat16), "col", scatter_dimension=0, tiled=True
        ).astype(jnp.float32),
        lax.psum_scatter(
            grad_values_part.astype(jnp.bfloat16), "col", scatter_dimension=0, tiled=True
        ).astype(jnp.float32),
    )
    grad_q = rotary_back(grad_queries.reshape(head_rows, query_heads, HD), cosine, sine).reshape(
        head_rows, query_width
    )
    grad_k = rotary_back(grad_keys, cosine, sine).reshape(head_rows, key_width)
    grad_v = grad_values.reshape(head_rows, key_width)
    grad_projected = jnp.concatenate([grad_q, grad_k, grad_v], axis=1).astype(jnp.bfloat16)
    grad_projected_all = spread_cols(grad_projected)
    bias_part = jnp.sum(grad_projected_all, axis=0, dtype=jnp.float32)
    grad_normed1 = across_rows(grad_projected_all, joint_weight, True, local_rows)
    back_first, gain1_part = norm_backward(grad_normed1, inputs, inverse1, norm1_gain)
    input_grad = (grad_hidden + back_first).astype(jnp.bfloat16)
    def row_pair(values):
        size = lax.axis_size("row")
        return values + lax.ppermute(values, "row", [(i, (i + 1) % size) for i in range(size)])

    line = lax.axis_size("dp") // 2
    feature_width = inputs.shape[1]
    gains = row_pair(jnp.concatenate([gain1_part, gain2_part]))
    small = jnp.concatenate([gains, bias_part])
    small = small + swap_pair(small)
    small_length = small.shape[0]
    small = jnp.pad(small, (0, -small_length % 1024)).reshape(-1, 128)
    rhs_both = jnp.concatenate([grad_both_all, spread_cols(swap_pair(grad_both))], 0)
    padding = ((0, 0), (0, 2 * key_width))
    gate_up_total, down_final, joint_total, small_total = line_totals(
        line,
        (
            pair_left(normed2_all),
            rhs_both,
            pair_left(activated_all),
            pair_right(grad_output_all),
            pair_left(mixed_all),
            jnp.pad(pair_right(grad_branch_all), padding),
            pair_left(normed1_all),
            pair_right(grad_projected_all),
            small,
        ),
    )
    block = feature_width // (2 * line)
    gate_final, up_final = gate_up_total[:block], gate_up_total[block:]
    output_final, joint_final = joint_total[:block, :query_width], joint_total[block:]
    query_final = joint_final[:, :query_width]
    key_final = joint_final[:, query_width : query_width + key_width]
    value_final = joint_final[:, query_width + key_width :]
    small_flat = small_total.reshape(-1)
    cuts = [feature_width, feature_width, query_width, key_width, key_width]
    ends = [sum(cuts[: i + 1]) for i in range(len(cuts))]
    gain1_final, gain2_final, qbias_final, kbias_final, vbias_final = (
        small_flat[end - cut : end] for end, cut in zip(ends, cuts)
    )
    return (
        output,
        input_grad,
        gain1_final,
        query_final,
        qbias_final,
        key_final,
        kbias_final,
        value_final,
        vbias_final,
        output_final,
        gain2_final,
        gate_final,
        up_final,
        down_final,
    )


def solution(mesh):
    placed = (
        P(("dp", "row"), "col"),
        P("dp", None),
        P(("dp", "row"), "col"),
        P("col"),
        P("col", "row"),
        P("row"),
        P("col", "row"),
        P("row"),
        P("col", "row"),
        P("row"),
        P("row", "col"),
        P("col"),
        P("col", "row"),
        P("col", "row"),
        P("row", "col"),
    )
    return jax.shard_map(
        per_device,
        mesh=mesh,
        in_specs=placed,
        out_specs=(
            P(("dp", "row"), "col"),
            P(("dp", "row"), "col"),
            P("col"),
            P(("col", "dp"), "row"),
            P("row"),
            P(("col", "dp"), "row"),
            P("row"),
            P(("col", "dp"), "row"),
            P("row"),
            P(("row", "dp"), "col"),
            P("col"),
            P(("col", "dp"), "row"),
            P(("col", "dp"), "row"),
            P(("row", "dp"), "col"),
        ),
        check_vma=False,
    )
```

```python
import functools

import jax
import jax.numpy as jnp
from jax import lax
from jax.experimental import pallas as pl
from jax.experimental.pallas import tpu as pltpu
from jax.sharding import PartitionSpec as P

D = 896
HD = 64
MESH = pl.DeviceIdType.MESH


NEGATIVE = -1e30
EPSILON = 1e-06
ROTARY_BASE = 1000000.0


def sequence_tables(lengths, group_rows):
    seq_ends = jnp.cumsum(lengths)
    seq_starts = seq_ends - lengths
    places = jnp.arange(group_rows, dtype=jnp.int32)
    segment = jnp.sum((places[:, None] >= seq_ends[None, :]).astype(jnp.int32), axis=1)
    member = segment[:, None] == jnp.arange(lengths.shape[0], dtype=jnp.int32)[None, :]
    position = places - jnp.sum(jnp.where(member, seq_starts[None, :], 0), axis=1)
    return (places, segment, position)


def rotary_tables(position):
    half_width = HD // 2
    frequency = ROTARY_BASE ** (-(jnp.arange(half_width, dtype=jnp.float32) * 2.0 / HD))
    angle = position.astype(jnp.float32)[:, None] * frequency[None, :]
    cosine = jnp.cos(angle)
    sine = jnp.sin(angle)
    return (
        jnp.concatenate([cosine, cosine], 1),
        jnp.concatenate([sine, sine], 1),
    )


def line_kernel(
    line,
    lhs_second,
    rhs_both,
    lhs_down,
    rhs_down,
    lhs_mixed,
    rhs_branch,
    lhs_first,
    rhs_projected,
    small_part,
    gate_up_out,
    down_out,
    joint_out,
    small_out,
    *scratch,
):
    send, below, above = scratch[0:3], scratch[3:6], scratch[6:9]
    small_send, small_below, small_above = scratch[9:12]
    send_sem, below_sem, above_sem, small_sem = scratch[12:16]
    index = lax.axis_index("dp")
    place = index // 2
    has_below = place > 0
    has_above = place < line - 1
    lower = {"dp": lax.rem(index + 2 * line - 2, 2 * line)}
    upper = {"dp": lax.rem(index + 2, 2 * line)}
    hidden_width = rhs_both.shape[1] // 2

    barrier = pltpu.get_barrier_semaphore()

    @pl.when(has_below)
    def _():
        pl.semaphore_signal(barrier, inc=1, device_id=lower, device_id_type=MESH)

    @pl.when(has_above)
    def _():
        pl.semaphore_signal(barrier, inc=1, device_id=upper, device_id_type=MESH)

    pl.semaphore_wait(barrier, has_below.astype(jnp.int32) + has_above.astype(jnp.int32))

    def term(piece, target):
        def dot(left, right):
            return jnp.dot(left, right, preferred_element_type=jnp.float32)

        if piece == 0:
            left = lhs_second[target]
            return jnp.concatenate(
                [dot(left, rhs_both[:, :hidden_width]), dot(left, rhs_both[:, hidden_width:])], 0
            )
        if piece == 1:
            return dot(lhs_down[target], rhs_down[...])
        return jnp.concatenate(
            [dot(lhs_mixed[target], rhs_branch[...]), dot(lhs_first[target], rhs_projected[...])], 0
        )

    outs = (gate_up_out, down_out, joint_out)

    def copy_up(piece, target):
        return pltpu.make_async_remote_copy(
            src_ref=send[piece].at[target],
            dst_ref=below[piece].at[target],
            send_sem=send_sem.at[piece, target],
            recv_sem=below_sem.at[piece, target],
            device_id=upper,
            device_id_type=MESH,
        )

    def copy_down(piece, target):
        return pltpu.make_async_remote_copy(
            src_ref=send[piece].at[target],
            dst_ref=above[piece].at[target],
            send_sem=send_sem.at[piece, target],
            recv_sem=above_sem.at[piece, target],
            device_id=lower,
            device_id_type=MESH,
        )

    def small_copy(source, landing, at, device):
        return pltpu.make_async_remote_copy(
            src_ref=source,
            dst_ref=landing,
            send_sem=small_sem.at[at],
            recv_sem=small_sem.at[at + 1],
            device_id=device,
            device_id_type=MESH,
        )

    small_up = small_copy(small_send.at[0], small_below, 0, upper)
    small_down = small_copy(small_send.at[1], small_above, 2, lower)

    @pl.when(jnp.logical_not(has_below))
    def _():
        small_below[...] = jnp.zeros_like(small_below)

    @pl.when(has_below)
    def _():
        small_up.wait_recv()

    @pl.when(has_above)
    def _():
        small_send[0] = small_below[...] + small_part[...]
        small_up.start()

    @pl.when(jnp.logical_not(has_above))
    def _():
        small_above[...] = jnp.zeros_like(small_above)

    def step(count, carry):
        half = count // 2
        target = jnp.where(count % 2 == 0, line - 1 - half, half)
        for piece in range(3):

            @pl.when(target > place)
            def _():
                own = term(piece, target)

                @pl.when(has_below)
                def _():
                    copy_up(piece, target).wait_recv()
                    send[piece][target] = (own + below[piece][target].astype(jnp.float32)).astype(
                        jnp.bfloat16
                    )

                @pl.when(jnp.logical_not(has_below))
                def _():
                    send[piece][target] = own.astype(jnp.bfloat16)

                copy_up(piece, target).start()

            @pl.when(target < place)
            def _():
                own = term(piece, target)

                @pl.when(has_above)
                def _():
                    copy_down(piece, target).wait_recv()
                    send[piece][target] = (own + above[piece][target].astype(jnp.float32)).astype(
                        jnp.bfloat16
                    )

                @pl.when(jnp.logical_not(has_above))
                def _():
                    send[piece][target] = own.astype(jnp.bfloat16)

                copy_down(piece, target).start()

            @pl.when(target == place)
            def _():
                outs[piece][...] = term(piece, target)

        return carry

    lax.fori_loop(0, line, step, 0)

    @pl.when(has_above)
    def _():
        small_down.wait_recv()

    @pl.when(has_below)
    def _():
        small_send[1] = small_above[...] + small_part[...]
        small_down.start()

    small_out[...] = small_below[...] + small_part[...] + small_above[...]

    for piece in range(3):

        @pl.when(has_below)
        def _():
            copy_up(piece, place).wait_recv()
            outs[piece][...] += below[piece][place].astype(jnp.float32)

        @pl.when(has_above)
        def _():
            copy_down(piece, place).wait_recv()
            outs[piece][...] += above[piece][place].astype(jnp.float32)

    def finish(target, carry):
        for piece in range(3):

            @pl.when(target != place)
            def _():
                copy_up(piece, target).wait_send()

        return carry

    lax.fori_loop(0, line, finish, 0)

    @pl.when(has_above)
    def _():
        small_up.wait_send()

    @pl.when(has_below)
    def _():
        small_down.wait_send()


def line_totals(line, operands):
    lhs_second, rhs_both, lhs_down, rhs_down, lhs_mixed, rhs_branch, _, rhs_projected, small = (
        operands
    )
    shapes = (
        (2 * lhs_second.shape[1], rhs_both.shape[1] // 2),
        (lhs_down.shape[1], rhs_down.shape[1]),
        (2 * lhs_mixed.shape[1], rhs_projected.shape[1]),
    )
    slots = [pltpu.VMEM((line,) + shape, jnp.bfloat16) for shape in shapes]
    vmem = pl.BlockSpec(memory_space=pltpu.VMEM)
    return pl.pallas_call(
        functools.partial(line_kernel, line),
        out_shape=[jax.ShapeDtypeStruct(shape, jnp.float32) for shape in shapes]
        + [jax.ShapeDtypeStruct(small.shape, jnp.float32)],
        in_specs=[vmem] * 9,
        out_specs=[vmem] * 4,
        scratch_shapes=slots * 3
        + [
            pltpu.VMEM((2,) + small.shape, jnp.float32),
            pltpu.VMEM(small.shape, jnp.float32),
            pltpu.VMEM(small.shape, jnp.float32),
            pltpu.SemaphoreType.DMA((3, line)),
            pltpu.SemaphoreType.DMA((3, line)),
            pltpu.SemaphoreType.DMA((3, line)),
            pltpu.SemaphoreType.DMA((4,)),
        ],
        compiler_params=pltpu.CompilerParams(
            collective_id=0, has_side_effects=True, vmem_limit_bytes=56 * 1024 * 1024
        ),
    )(*operands)


def swap_pair(values):
    count = lax.axis_size("dp")
    return lax.ppermute(values, "dp", [(i, i ^ 1) for i in range(count)])


def layer_kernel(
    tokens, cotangent, gain1, joint, joint_bias, o_weight, gain2, gate_weight, up_weight,
    down_weight, cosine, sine, allowed,
    output, input_grad, small_out,
    first_f, mixed_f, second_f, active_f, cot_f, both_f, branch_f, projected_f,
    joint_peer, o_peer, gate_peer, up_peer, down_peer, gains_peer,
    raw_row, raw_send, raw_col, kv, first_oth, second_oth, branch_oth,
    sum_send, sum_recv, kv_send, kv_recv, out_send, out_recv, send_sem, recv_sem,
):
    row, col, pair = lax.axis_index("row"), lax.axis_index("col"), lax.axis_index("dp")
    row_peer, col_peer = {"row": 1 - row}, {"col": 1 - col}
    x_peer = {"dp": pair + 1 - 2 * lax.rem(pair, 2)}
    f32, b16 = jnp.float32, jnp.bfloat16
    rows, half = tokens.shape
    width = 2 * half
    query_width = o_weight.shape[0]
    key_width = (joint.shape[1] - query_width) // 2
    heads = query_width // HD
    hidden_width = gate_weight.shape[1]
    scale = HD ** (-0.5)
    started = []

    def copy(source, target, device):
        at = len(started)
        made = pltpu.make_async_remote_copy(
            src_ref=source,
            dst_ref=target,
            send_sem=send_sem.at[at],
            recv_sem=recv_sem.at[at],
            device_id=device,
            device_id_type=MESH,
        )
        made.start()
        started.append(made)
        return made

    def dot(left, right):
        return jnp.dot(left, right, preferred_element_type=f32)

    def dot_back(left, right):
        return lax.dot_general(left, right, (((1,), (1,)), ((), ())), preferred_element_type=f32)

    def dot_outer(left, right):
        return lax.dot_general(left, right, (((0,), (0,)), ((), ())), preferred_element_type=f32)

    barrier = pltpu.get_barrier_semaphore()
    for device in (row_peer, col_peer, x_peer):
        pl.semaphore_signal(barrier, inc=1, device_id=device, device_id_type=MESH)
    pl.semaphore_wait(barrier, 3)

    got_raw = [
        copy(tokens, raw_row.at[0], row_peer),
        copy(cotangent, raw_row.at[1], row_peer),
    ]
    got_joint = copy(joint, joint_peer, col_peer)
    gains_peer[0] = gain1[...]
    gains_peer[1] = gain2[...]
    got_gains = copy(gains_peer.at[pl.ds(0, 2)], gains_peer.at[pl.ds(2, 2)], col_peer)
    diagonal = row == col
    token_own = []
    got_col = []
    for i, source in enumerate((tokens, cotangent)):
        got_raw[i].wait_recv()
        token_own.append(jnp.where(diagonal, source[...], raw_row[i]))
        raw_send[i] = jnp.where(diagonal, raw_row[i], source[...])
        got_col.append(copy(raw_send.at[i], raw_col.at[i], col_peer))
    got_o = copy(o_weight, o_peer, col_peer)
    got_gate = copy(gate_weight, gate_peer, col_peer)
    got_up = copy(up_weight, up_peer, col_peer)
    got_down = copy(down_weight, down_peer, col_peer)
    got_gains.wait_recv()
    gain1_own, gain1_oth = gain1[...], gains_peer[2]
    gain2_own, gain2_oth = gain2[...], gains_peer[3]

    def total(own, oth):
        return jnp.sum(own, axis=1, keepdims=True) + jnp.sum(oth, axis=1, keepdims=True)

    def norm_pair(own, oth):
        return lax.rsqrt(total(own * own, oth * oth) / width + EPSILON)

    later = []

    def split_factor(factor):
        later.append(copy(factor.at[0], factor.at[2], x_peer))
        return factor

    def split_rest(factor, got):
        got.wait_recv()
        later.append(copy(factor.at[1], factor.at[3], x_peer))

    def shared_factor(factor):
        later.append(copy(factor.at[0], factor.at[1], col_peer))
        got = copy(factor.at[0], factor.at[2], x_peer)
        return got

    def shared_rest(factor, got):
        got.wait_recv()
        later.append(copy(factor.at[2], factor.at[3], col_peer))

    tok_own = token_own[0].astype(f32)
    cot_f[0] = token_own[1]
    cot_f[1] = raw_send[1]
    later.append(copy(cot_f.at[pl.ds(0, 2)], cot_f.at[pl.ds(2, 2)], x_peer))
    got_col[0].wait_recv()
    tok_oth = raw_col[0].astype(f32)
    inverse1 = norm_pair(tok_own, tok_oth)
    first_f[0] = (tok_own * inverse1 * gain1_own).astype(b16)
    first_oth[...] = (tok_oth * inverse1 * gain1_oth).astype(b16)
    got_first = copy(first_oth, first_f.at[1], col_peer)
    split_factor(first_f)
    got_joint.wait_recv()
    projected = dot(first_f[0], joint[...]) + dot(first_oth[...], joint_peer[...])
    projected = projected + joint_bias[...]
    turn_width = query_width + key_width
    lane = lax.broadcasted_iota(jnp.int32, (rows, turn_width), 1)
    first_half = lax.rem(lane, HD) < HD // 2

    def turned(values):
        return jnp.where(
            first_half,
            -pltpu.roll(values, turn_width - HD // 2, 1),
            pltpu.roll(values, HD // 2, 1),
        )

    straight = projected[:, :turn_width]
    spun = (straight * cosine[...] + turned(straight) * sine[...]).astype(b16)
    kv[0, :, :key_width] = spun[:, query_width:]
    kv[0, :, key_width:] = projected[:, turn_width:].astype(b16)
    got_kv = copy(kv.at[0], kv.at[1], col_peer)

    def stack(values):
        return jnp.concatenate([values[:, h * HD : (h + 1) * HD] for h in range(heads)], 0)

    def unstack(values):
        return jnp.concatenate([values[h * rows : (h + 1) * rows] for h in range(heads)], 1)

    queries = stack(spun)
    split_rest(first_f, got_first)
    got_kv.wait_recv()
    keys = jnp.concatenate([kv[0, :, :key_width], kv[1, :, :key_width]], 0)
    values = jnp.concatenate([kv[0, :, key_width:], kv[1, :, key_width:]], 0)
    mask = jnp.concatenate([allowed[...]] * heads, 0) > 0.5
    scores = jnp.where(mask, dot_back(queries, keys) * scale, NEGATIVE)
    raised = jnp.exp(scores - jnp.max(scores, axis=1, keepdims=True))
    exact = raised / jnp.sum(raised, axis=1, keepdims=True)
    probs = exact.astype(b16)
    mixed_f[0] = unstack(dot(probs, values)).astype(b16)
    got_mixed = shared_factor(mixed_f)
    got_o.wait_recv()

    def across_rows(at, own, oth):
        sum_send[at, 0] = own.astype(b16)
        sum_send[at, 1] = oth.astype(b16)
        got = copy(sum_send.at[at], sum_recv.at[at], row_peer)
        return got

    own_part, oth_part = dot(mixed_f[0], o_weight[...]), dot(mixed_f[0], o_peer[...])
    got = across_rows(0, own_part, oth_part)
    shared_rest(mixed_f, got_mixed)
    got_down.wait_recv()
    got_col[1].wait_recv()
    grad_activated = dot_back(cot_f[0], down_weight[...]) + dot_back(raw_col[1], down_peer[...])
    got.wait_recv()
    hidden_own = tok_own + (own_part + sum_recv[0, 0].astype(f32))
    hidden_oth = tok_oth + (oth_part + sum_recv[0, 1].astype(f32))

    inverse2 = norm_pair(hidden_own, hidden_oth)
    second_f[0] = (hidden_own * inverse2 * gain2_own).astype(b16)
    second_oth[...] = (hidden_oth * inverse2 * gain2_oth).astype(b16)
    got_second = copy(second_oth, second_f.at[1], col_peer)
    split_factor(second_f)
    got_gate.wait_recv()
    gate_value = dot(second_f[0], gate_weight[...]) + dot(second_oth[...], gate_peer[...])
    got_up.wait_recv()
    up_value = dot(second_f[0], up_weight[...]) + dot(second_oth[...], up_peer[...])
    sigmoid_value = 1.0 / (1.0 + jnp.exp(-gate_value))
    silu_value = gate_value * sigmoid_value
    active_f[0] = (silu_value * up_value).astype(b16)
    grad_gate = (
        grad_activated * up_value * (sigmoid_value * (1.0 + gate_value * (1.0 - sigmoid_value)))
    ).astype(b16)
    grad_up = (grad_activated * silu_value).astype(b16)
    both_f[0, :, :hidden_width] = grad_gate
    both_f[0, :, hidden_width:] = grad_up
    back_own = dot_back(grad_gate, gate_weight[...]) + dot_back(grad_up, up_weight[...])
    back_oth = dot_back(grad_gate, gate_peer[...]) + dot_back(grad_up, up_peer[...])
    got_back = across_rows(1, back_own, back_oth)
    got_both = shared_factor(both_f)
    got_active = shared_factor(active_f)
    split_rest(second_f, got_second)
    out_own, out_oth = dot(active_f[0], down_weight[...]), dot(active_f[0], down_peer[...])
    got_out = across_rows(2, out_own, out_oth)
    got_back.wait_recv()
    back_own = back_own + sum_recv[1, 0].astype(f32)
    back_oth = back_oth + sum_recv[1, 1].astype(f32)

    def norm_back(grad_own, grad_oth, own, oth, inverse, gain_own, gain_oth):
        weighted_own, weighted_oth = grad_own * gain_own, grad_oth * gain_oth
        factor = inverse * inverse * inverse * total(weighted_own * own, weighted_oth * oth) / width
        return (
            weighted_own * inverse - own * factor,
            weighted_oth * inverse - oth * factor,
            jnp.sum(grad_own * own * inverse, axis=0, keepdims=True),
            jnp.sum(grad_oth * oth * inverse, axis=0, keepdims=True),
        )

    hid_own, hid_oth, gain2_part, gain2_rest = norm_back(
        back_own, back_oth, hidden_own, hidden_oth, inverse2, gain2_own, gain2_oth
    )
    hid_own = hid_own + token_own[1].astype(f32)
    hid_oth = hid_oth + raw_col[1].astype(f32)

    branch_f[0] = hid_own.astype(b16)
    branch_oth[...] = hid_oth.astype(b16)
    got_branch = copy(branch_oth, branch_f.at[1], col_peer)
    split_factor(branch_f)
    grad_mixed = (
        dot_back(branch_f[0], o_weight[...]) + dot_back(branch_oth[...], o_peer[...])
    ).astype(b16)
    grad_stack = stack(grad_mixed)
    grad_probs = dot_back(grad_stack, values)
    grad_scores = exact * (grad_probs - jnp.sum(grad_probs * exact, axis=1, keepdims=True))
    grad_scores = grad_scores.astype(b16)
    grad_keys = dot_outer(grad_scores, queries) * scale
    grad_values = dot_outer(probs, grad_stack)
    kv_send[:, :key_width] = grad_keys[rows:].astype(b16)
    kv_send[:, key_width:] = grad_values[rows:].astype(b16)
    got_kv = copy(kv_send, kv_recv, col_peer)
    grad_queries = unstack(dot(grad_scores, keys)) * scale
    split_rest(branch_f, got_branch)
    got_kv.wait_recv()
    grad_keys = grad_keys[:rows] + kv_recv[:, :key_width].astype(f32)
    grad_values = grad_values[:rows] + kv_recv[:, key_width:].astype(f32)
    turn_grad = jnp.concatenate([grad_queries, grad_keys], 1)
    turn_grad = turn_grad * cosine[...] - turned(turn_grad * sine[...])
    projected_f[0] = jnp.concatenate([turn_grad, grad_values], 1).astype(b16)
    part_own = dot_back(projected_f[0], joint[...])
    part_oth = dot_back(projected_f[0], joint_peer[...])
    got_in = across_rows(3, part_own, part_oth)
    got_projected = shared_factor(projected_f)

    got_out.wait_recv()
    out_own = hidden_own + (out_own + sum_recv[2, 0].astype(f32))
    out_oth = hidden_oth + (out_oth + sum_recv[2, 1].astype(f32))
    out_send[0] = out_oth.astype(b16)
    got_output = copy(out_send.at[0], out_recv.at[0], col_peer)
    got_in.wait_recv()
    part_own = part_own + sum_recv[3, 0].astype(f32)
    part_oth = part_oth + sum_recv[3, 1].astype(f32)
    in_own, in_oth, gain1_part, gain1_rest = norm_back(
        part_own, part_oth, tok_own, tok_oth, inverse1, gain1_own, gain1_oth
    )
    in_own = hid_own + in_own
    in_oth = hid_oth + in_oth
    out_send[1] = in_oth.astype(b16)
    got_input = copy(out_send.at[1], out_recv.at[1], col_peer)
    small_out[0:1, :half] = gain1_part
    small_out[1:2, :half] = gain1_rest
    small_out[2:3, :half] = gain2_part
    small_out[3:4, :half] = gain2_rest
    small_out[4:5, :] = jnp.sum(projected_f[0].astype(f32), axis=0, keepdims=True)
    shared_rest(both_f, got_both)
    shared_rest(active_f, got_active)
    shared_rest(projected_f, got_projected)
    got_output.wait_recv()
    output[...] = jnp.where(diagonal, out_own.astype(b16), out_recv[0])
    got_input.wait_recv()
    input_grad[...] = jnp.where(diagonal, in_own.astype(b16), out_recv[1])
    for made in later:
        made.wait_recv()
    for made in started:
        made.wait_send()


def layer_pass(tokens, joint, o_weight, gate_weight, rest):
    rows, half = tokens.shape
    query_width, hidden_width, joint_width = o_weight.shape[0], gate_weight.shape[1], joint.shape[1]
    key_width = (joint_width - query_width) // 2
    b16, f32 = jnp.bfloat16, jnp.float32

    def blocks(width):
        return jax.ShapeDtypeStruct((4, rows, width), b16)

    vmem = pl.BlockSpec(memory_space=pltpu.VMEM)
    outs = [
        jax.ShapeDtypeStruct((rows, half), b16),
        jax.ShapeDtypeStruct((rows, half), b16),
        jax.ShapeDtypeStruct((8, joint_width), f32),
        blocks(half),
        blocks(query_width),
        blocks(half),
        blocks(hidden_width),
        blocks(half),
        blocks(2 * hidden_width),
        blocks(half),
        blocks(joint_width),
    ]
    return pl.pallas_call(
        layer_kernel,
        out_shape=outs,
        in_specs=[vmem] * len(rest),
        out_specs=[vmem] * len(outs),
        scratch_shapes=[
            pltpu.VMEM((half, joint_width), b16),
            pltpu.VMEM((query_width, half), b16),
            pltpu.VMEM((half, hidden_width), b16),
            pltpu.VMEM((half, hidden_width), b16),
            pltpu.VMEM((hidden_width, half), b16),
            pltpu.VMEM((4, 1, half), f32),
            pltpu.VMEM((2, rows, half), b16),
            pltpu.VMEM((2, rows, half), b16),
            pltpu.VMEM((2, rows, half), b16),
            pltpu.VMEM((2, rows, 2 * key_width), b16),
            pltpu.VMEM((rows, half), b16),
            pltpu.VMEM((rows, half), b16),
            pltpu.VMEM((rows, half), b16),
            pltpu.VMEM((4, 2, rows, half), b16),
            pltpu.VMEM((4, 2, rows, half), b16),
            pltpu.VMEM((rows, 2 * key_width), b16),
            pltpu.VMEM((rows, 2 * key_width), b16),
            pltpu.VMEM((2, rows, half), b16),
            pltpu.VMEM((2, rows, half), b16),
            pltpu.SemaphoreType.DMA((48,)),
            pltpu.SemaphoreType.DMA((48,)),
        ],
        compiler_params=pltpu.CompilerParams(
            collective_id=1, has_side_effects=True, vmem_limit_bytes=60 * 1024 * 1024
        ),
    )(*rest)


def pair_left(blocks):
    line = lax.axis_size("dp") // 2
    columns = blocks.shape[2]
    parts = blocks.reshape(-1, line, 2, columns // (2 * line))
    mine = lax.dynamic_index_in_dim(parts, lax.axis_index("dp") % 2, 2, keepdims=False)
    return mine.transpose(1, 2, 0)


def pair_right(blocks):
    return blocks.reshape(-1, blocks.shape[2])


def per_device(
    tokens,
    seq_lengths,
    cotangent,
    norm1_gain,
    q_weight,
    q_bias,
    k_weight,
    k_bias,
    v_weight,
    v_bias,
    o_weight,
    norm2_gain,
    gate_weight,
    up_weight,
    down_weight,
):
    local_rows = tokens.shape[0]
    group_rows = local_rows * lax.axis_size("row")
    head_rows = group_rows // lax.axis_size("col")
    query_width = q_weight.shape[1]
    key_width = k_weight.shape[1]
    hidden_width = gate_weight.shape[1]
    places, segment, position = sequence_tables(seq_lengths[0], group_rows)
    block_start = lax.axis_index("col") * head_rows

    def from_own(table, how_many):
        return lax.dynamic_slice_in_dim(jnp.concatenate([table, table]), block_start, how_many, 0)

    own_places, own_segment = from_own(places, head_rows), from_own(segment, head_rows)
    key_places, key_segment = from_own(places, group_rows), from_own(segment, group_rows)
    allowed = (own_segment[:, None] == key_segment[None, :]) & (
        key_places[None, :] <= own_places[:, None]
    )
    cosine, sine = rotary_tables(from_own(position, head_rows))
    turn_heads = (query_width + key_width) // HD
    joint_weight = jnp.concatenate([q_weight, k_weight, v_weight], axis=1)
    joint_bias = jnp.concatenate([q_bias, k_bias, v_bias])
    (
        output,
        input_grad,
        small,
        first_f,
        mixed_f,
        second_f,
        active_f,
        cot_f,
        both_f,
        branch_f,
        projected_f,
    ) = layer_pass(
        tokens,
        joint_weight,
        o_weight,
        gate_weight,
        (
            tokens,
            cotangent,
            norm1_gain[None],
            joint_weight,
            joint_bias[None],
            o_weight,
            norm2_gain[None],
            gate_weight,
            up_weight,
            down_weight,
            jnp.tile(cosine, (1, turn_heads)),
            jnp.tile(sine, (1, turn_heads)),
            allowed.astype(jnp.float32),
        ),
    )
    feature_width = tokens.shape[1]
    sent = jnp.concatenate([small[1, :feature_width], small[3, :feature_width], small[4]])
    size = lax.axis_size("col")
    got = lax.ppermute(sent, "col", [(i, (i + 1) % size) for i in range(size)])
    kept = jnp.concatenate([small[0, :feature_width], small[2, :feature_width], small[4]])
    small = kept + got
    small = small + swap_pair(small)
    small = jnp.pad(small, (0, -small.shape[0] % 1024)).reshape(-1, 128)
    line = lax.axis_size("dp") // 2
    padding = ((0, 0), (0, 2 * key_width))
    gate_up_total, down_final, joint_total, small_total = line_totals(
        line,
        (
            pair_left(second_f),
            pair_right(both_f),
            pair_left(active_f),
            pair_right(cot_f),
            pair_left(mixed_f),
            jnp.pad(pair_right(branch_f), padding),
            pair_left(first_f),
            pair_right(projected_f),
            small,
        ),
    )
    block = feature_width // (2 * line)
    gate_final, up_final = gate_up_total[:block], gate_up_total[block:]
    output_final, joint_final = joint_total[:block, :query_width], joint_total[block:]
    query_final = joint_final[:, :query_width]
    key_final = joint_final[:, query_width : query_width + key_width]
    value_final = joint_final[:, query_width + key_width :]
    small_flat = small_total.reshape(-1)
    cuts = [feature_width, feature_width, query_width, key_width, key_width]
    ends = [sum(cuts[: i + 1]) for i in range(len(cuts))]
    gain1_final, gain2_final, qbias_final, kbias_final, vbias_final = (
        small_flat[end - cut : end] for end, cut in zip(ends, cuts)
    )
    return (
        output,
        input_grad,
        gain1_final,
        query_final,
        qbias_final,
        key_final,
        kbias_final,
        value_final,
        vbias_final,
        output_final,
        gain2_final,
        gate_final,
        up_final,
        down_final,
    )


def solution(mesh):
    placed = (
        P(("dp", "row"), "col"),
        P("dp", None),
        P(("dp", "row"), "col"),
        P("col"),
        P("col", "row"),
        P("row"),
        P("col", "row"),
        P("row"),
        P("col", "row"),
        P("row"),
        P("row", "col"),
        P("col"),
        P("col", "row"),
        P("col", "row"),
        P("row", "col"),
    )
    return jax.shard_map(
        per_device,
        mesh=mesh,
        in_specs=placed,
        out_specs=(
            P(("dp", "row"), "col"),
            P(("dp", "row"), "col"),
            P("col"),
            P(("col", "dp"), "row"),
            P("row"),
            P(("col", "dp"), "row"),
            P("row"),
            P(("col", "dp"), "row"),
            P("row"),
            P(("row", "dp"), "col"),
            P("col"),
            P(("col", "dp"), "row"),
            P(("col", "dp"), "row"),
            P(("row", "dp"), "col"),
        ),
        check_vma=False,
    )
```

```python
import functools

import jax
import jax.numpy as jnp
from jax import lax
from jax.experimental import pallas as pl
from jax.experimental.pallas import tpu as pltpu
from jax.sharding import PartitionSpec as P

D = 896
HD = 64
MESH = pl.DeviceIdType.MESH


NEGATIVE = -1e30
EPSILON = 1e-06
ROTARY_BASE = 1000000.0


def sequence_tables(lengths, group_rows):
    seq_ends = jnp.cumsum(lengths)
    seq_starts = seq_ends - lengths
    places = jnp.arange(group_rows, dtype=jnp.int32)
    segment = jnp.sum((places[:, None] >= seq_ends[None, :]).astype(jnp.int32), axis=1)
    member = segment[:, None] == jnp.arange(lengths.shape[0], dtype=jnp.int32)[None, :]
    position = places - jnp.sum(jnp.where(member, seq_starts[None, :], 0), axis=1)
    return (places, segment, position)


def rotary_tables(position):
    half_width = HD // 2
    frequency = ROTARY_BASE ** (-(jnp.arange(half_width, dtype=jnp.float32) * 2.0 / HD))
    angle = position.astype(jnp.float32)[:, None] * frequency[None, :]
    cosine = jnp.cos(angle)
    sine = jnp.sin(angle)
    return (
        jnp.concatenate([cosine, cosine], 1),
        jnp.concatenate([sine, sine], 1),
    )


def line_kernel(
    line,
    lhs_second,
    rhs_both,
    lhs_down,
    rhs_down,
    lhs_mixed,
    rhs_branch,
    lhs_first,
    rhs_projected,
    small_part,
    gate_up_out,
    down_out,
    joint_out,
    small_out,
    *scratch,
):
    send, below, above = scratch[0:3], scratch[3:6], scratch[6:9]
    small_send, small_below, small_above = scratch[9:12]
    send_sem, below_sem, above_sem, small_sem = scratch[12:16]
    index = lax.axis_index("dp")
    place = index // 2
    has_below = place > 0
    has_above = place < line - 1
    lower = {"dp": lax.rem(index + 2 * line - 2, 2 * line)}
    upper = {"dp": lax.rem(index + 2, 2 * line)}
    hidden_width = rhs_both.shape[1] // 2

    barrier = pltpu.get_barrier_semaphore()

    @pl.when(has_below)
    def _():
        pl.semaphore_signal(barrier, inc=1, device_id=lower, device_id_type=MESH)

    @pl.when(has_above)
    def _():
        pl.semaphore_signal(barrier, inc=1, device_id=upper, device_id_type=MESH)

    pl.semaphore_wait(barrier, has_below.astype(jnp.int32) + has_above.astype(jnp.int32))

    def term(piece, target):
        def dot(left, right):
            return jnp.dot(left, right, preferred_element_type=jnp.float32)

        def picked(factor):
            tokens, columns = factor.shape
            count = columns // (2 * line)
            shape = (count, columns)
            first = (2 * target + lax.rem(index, 2)) * count
            chosen = lax.broadcasted_iota(jnp.int32, shape, 1) == first + lax.broadcasted_iota(
                jnp.int32, shape, 0
            )
            return lax.dot_general(
                chosen.astype(jnp.float32).astype(jnp.bfloat16),
                factor[...],
                (((1,), (1,)), ((), ())),
                preferred_element_type=jnp.float32,
            ).astype(jnp.bfloat16)

        if piece == 0:
            left = picked(lhs_second)
            return jnp.concatenate(
                [dot(left, rhs_both[:, :hidden_width]), dot(left, rhs_both[:, hidden_width:])], 0
            )
        if piece == 1:
            return dot(picked(lhs_down), rhs_down[...])
        return jnp.concatenate(
            [dot(picked(lhs_mixed), rhs_branch[...]), dot(picked(lhs_first), rhs_projected[...])], 0
        )

    outs = (gate_up_out, down_out, joint_out)

    def copy_up(piece, target):
        return pltpu.make_async_remote_copy(
            src_ref=send[piece].at[target],
            dst_ref=below[piece].at[target],
            send_sem=send_sem.at[piece, target],
            recv_sem=below_sem.at[piece, target],
            device_id=upper,
            device_id_type=MESH,
        )

    def copy_down(piece, target):
        return pltpu.make_async_remote_copy(
            src_ref=send[piece].at[target],
            dst_ref=above[piece].at[target],
            send_sem=send_sem.at[piece, target],
            recv_sem=above_sem.at[piece, target],
            device_id=lower,
            device_id_type=MESH,
        )

    def small_copy(source, landing, at, device):
        return pltpu.make_async_remote_copy(
            src_ref=source,
            dst_ref=landing,
            send_sem=small_sem.at[at],
            recv_sem=small_sem.at[at + 1],
            device_id=device,
            device_id_type=MESH,
        )

    small_up = small_copy(small_send.at[0], small_below, 0, upper)
    small_down = small_copy(small_send.at[1], small_above, 2, lower)

    @pl.when(jnp.logical_not(has_below))
    def _():
        small_below[...] = jnp.zeros_like(small_below)

    @pl.when(has_below)
    def _():
        small_up.wait_recv()

    @pl.when(has_above)
    def _():
        small_send[0] = small_below[...] + small_part[...]
        small_up.start()

    @pl.when(jnp.logical_not(has_above))
    def _():
        small_above[...] = jnp.zeros_like(small_above)

    def step(count, carry):
        half = count // 2
        target = jnp.where(count % 2 == 0, line - 1 - half, half)
        for piece in range(3):

            @pl.when(target > place)
            def _():
                own = term(piece, target)

                @pl.when(has_below)
                def _():
                    copy_up(piece, target).wait_recv()
                    send[piece][target] = (own + below[piece][target].astype(jnp.float32)).astype(
                        jnp.bfloat16
                    )

                @pl.when(jnp.logical_not(has_below))
                def _():
                    send[piece][target] = own.astype(jnp.bfloat16)

                copy_up(piece, target).start()

            @pl.when(target < place)
            def _():
                own = term(piece, target)

                @pl.when(has_above)
                def _():
                    copy_down(piece, target).wait_recv()
                    send[piece][target] = (own + above[piece][target].astype(jnp.float32)).astype(
                        jnp.bfloat16
                    )

                @pl.when(jnp.logical_not(has_above))
                def _():
                    send[piece][target] = own.astype(jnp.bfloat16)

                copy_down(piece, target).start()

            @pl.when(target == place)
            def _():
                outs[piece][...] = term(piece, target)

        return carry

    lax.fori_loop(0, line, step, 0)

    @pl.when(has_above)
    def _():
        small_down.wait_recv()

    @pl.when(has_below)
    def _():
        small_send[1] = small_above[...] + small_part[...]
        small_down.start()

    small_out[...] = small_below[...] + small_part[...] + small_above[...]

    for piece in range(3):

        @pl.when(has_below)
        def _():
            copy_up(piece, place).wait_recv()
            outs[piece][...] += below[piece][place].astype(jnp.float32)

        @pl.when(has_above)
        def _():
            copy_down(piece, place).wait_recv()
            outs[piece][...] += above[piece][place].astype(jnp.float32)

    def finish(target, carry):
        for piece in range(3):

            @pl.when(target != place)
            def _():
                copy_up(piece, target).wait_send()

        return carry

    lax.fori_loop(0, line, finish, 0)

    @pl.when(has_above)
    def _():
        small_up.wait_send()

    @pl.when(has_below)
    def _():
        small_down.wait_send()


def line_totals(line, operands):
    lhs_second, rhs_both, lhs_down, rhs_down, lhs_mixed, rhs_branch, _, rhs_projected, small = (
        operands
    )
    shapes = (
        (lhs_second.shape[1] // line, rhs_both.shape[1] // 2),
        (lhs_down.shape[1] // (2 * line), rhs_down.shape[1]),
        (lhs_mixed.shape[1] // line, rhs_projected.shape[1]),
    )
    slots = [pltpu.VMEM((line,) + shape, jnp.bfloat16) for shape in shapes]
    vmem = pl.BlockSpec(memory_space=pltpu.VMEM)
    return pl.pallas_call(
        functools.partial(line_kernel, line),
        out_shape=[jax.ShapeDtypeStruct(shape, jnp.float32) for shape in shapes]
        + [jax.ShapeDtypeStruct(small.shape, jnp.float32)],
        in_specs=[vmem] * 9,
        out_specs=[vmem] * 4,
        scratch_shapes=slots * 3
        + [
            pltpu.VMEM((2,) + small.shape, jnp.float32),
            pltpu.VMEM(small.shape, jnp.float32),
            pltpu.VMEM(small.shape, jnp.float32),
            pltpu.SemaphoreType.DMA((3, line)),
            pltpu.SemaphoreType.DMA((3, line)),
            pltpu.SemaphoreType.DMA((3, line)),
            pltpu.SemaphoreType.DMA((4,)),
        ],
        compiler_params=pltpu.CompilerParams(
            collective_id=0, has_side_effects=True, vmem_limit_bytes=56 * 1024 * 1024
        ),
    )(*operands)


def layer_kernel(
    tokens, cotangent, gain1, joint, joint_bias, o_weight, gain2, gate_weight, up_weight,
    down_weight, cosine, sine, allowed,
    output, input_grad, small_out,
    first_f, mixed_f, second_f, active_f, cot_f, both_f, branch_f, projected_f,
    joint_peer, o_peer, gate_peer, up_peer, down_peer, gains_peer,
    raw_row, raw_send, raw_col, kv, first_oth, second_oth, branch_oth,
    sum_send, sum_recv, kv_send, kv_recv, out_send, out_recv, small, small_got, send_sem, recv_sem,
):
    row, col, pair = lax.axis_index("row"), lax.axis_index("col"), lax.axis_index("dp")
    row_peer, col_peer = {"row": 1 - row}, {"col": 1 - col}
    x_peer = {"dp": pair + 1 - 2 * lax.rem(pair, 2)}
    f32, b16 = jnp.float32, jnp.bfloat16
    rows, half = tokens.shape
    width = 2 * half
    query_width = o_weight.shape[0]
    key_width = (joint.shape[1] - query_width) // 2
    heads = query_width // HD
    hidden_width = gate_weight.shape[1]
    scale = HD ** (-0.5)
    started = []

    def copy(source, target, device):
        at = len(started)
        made = pltpu.make_async_remote_copy(
            src_ref=source,
            dst_ref=target,
            send_sem=send_sem.at[at],
            recv_sem=recv_sem.at[at],
            device_id=device,
            device_id_type=MESH,
        )
        made.start()
        started.append(made)
        return made

    def dot(left, right):
        return jnp.dot(left, right, preferred_element_type=f32)

    def dot_back(left, right):
        return lax.dot_general(left, right, (((1,), (1,)), ((), ())), preferred_element_type=f32)

    def dot_outer(left, right):
        return lax.dot_general(left, right, (((0,), (0,)), ((), ())), preferred_element_type=f32)

    barrier = pltpu.get_barrier_semaphore()
    for device in (row_peer, col_peer, x_peer):
        pl.semaphore_signal(barrier, inc=1, device_id=device, device_id_type=MESH)
    pl.semaphore_wait(barrier, 3)

    got_raw = [
        copy(tokens, raw_row.at[0], row_peer),
        copy(cotangent, raw_row.at[1], row_peer),
    ]
    got_joint = copy(joint, joint_peer, col_peer)
    gains_peer[0] = gain1[...]
    gains_peer[1] = gain2[...]
    got_gains = copy(gains_peer.at[pl.ds(0, 2)], gains_peer.at[pl.ds(2, 2)], col_peer)
    diagonal = row == col
    token_own = []
    got_col = []
    for i, source in enumerate((tokens, cotangent)):
        got_raw[i].wait_recv()
        token_own.append(jnp.where(diagonal, source[...], raw_row[i]))
        raw_send[i] = jnp.where(diagonal, raw_row[i], source[...])
        got_col.append(copy(raw_send.at[i], raw_col.at[i], col_peer))
    got_o = copy(o_weight, o_peer, col_peer)
    got_gate = copy(gate_weight, gate_peer, col_peer)
    got_up = copy(up_weight, up_peer, col_peer)
    got_down = copy(down_weight, down_peer, col_peer)
    got_gains.wait_recv()
    gain1_own, gain1_oth = gain1[...], gains_peer[2]
    gain2_own, gain2_oth = gain2[...], gains_peer[3]

    def total(own, oth):
        return jnp.sum(own, axis=1, keepdims=True) + jnp.sum(oth, axis=1, keepdims=True)

    def norm_pair(own, oth):
        return lax.rsqrt(total(own * own, oth * oth) / width + EPSILON)

    later = []

    def split_factor(factor):
        later.append(copy(factor.at[0], factor.at[2], x_peer))
        return factor

    def split_rest(factor, got):
        got.wait_recv()
        later.append(copy(factor.at[1], factor.at[3], x_peer))

    def shared_factor(factor):
        later.append(copy(factor.at[0], factor.at[1], col_peer))
        got = copy(factor.at[0], factor.at[2], x_peer)
        return got

    def shared_rest(factor, got):
        got.wait_recv()
        later.append(copy(factor.at[2], factor.at[3], col_peer))

    tok_own = token_own[0].astype(f32)
    cot_f[0] = token_own[1]
    cot_f[1] = raw_send[1]
    later.append(copy(cot_f.at[pl.ds(0, 2)], cot_f.at[pl.ds(2, 2)], x_peer))
    got_col[0].wait_recv()
    tok_oth = raw_col[0].astype(f32)
    inverse1 = norm_pair(tok_own, tok_oth)
    first_f[0] = (tok_own * inverse1 * gain1_own).astype(b16)
    first_oth[...] = (tok_oth * inverse1 * gain1_oth).astype(b16)
    got_first = copy(first_oth, first_f.at[1], col_peer)
    split_factor(first_f)
    got_joint.wait_recv()
    projected = dot(first_f[0], joint[...]) + dot(first_oth[...], joint_peer[...])
    projected = projected + joint_bias[...]
    turn_width = query_width + key_width
    lane = lax.broadcasted_iota(jnp.int32, (rows, turn_width), 1)
    first_half = lax.rem(lane, HD) < HD // 2

    def turned(values):
        return jnp.where(
            first_half,
            -pltpu.roll(values, turn_width - HD // 2, 1),
            pltpu.roll(values, HD // 2, 1),
        )

    straight = projected[:, :turn_width]
    spun = (straight * cosine[...] + turned(straight) * sine[...]).astype(b16)
    kv[0, :, :key_width] = spun[:, query_width:]
    kv[0, :, key_width:] = projected[:, turn_width:].astype(b16)
    got_kv = copy(kv.at[0], kv.at[1], col_peer)

    def stack(values):
        return jnp.concatenate([values[:, h * HD : (h + 1) * HD] for h in range(heads)], 0)

    def unstack(values):
        return jnp.concatenate([values[h * rows : (h + 1) * rows] for h in range(heads)], 1)

    queries = stack(spun)
    split_rest(first_f, got_first)
    got_kv.wait_recv()
    keys = jnp.concatenate([kv[0, :, :key_width], kv[1, :, :key_width]], 0)
    values = jnp.concatenate([kv[0, :, key_width:], kv[1, :, key_width:]], 0)
    mask = jnp.concatenate([allowed[...]] * heads, 0) > 0.5
    scores = jnp.where(mask, dot_back(queries, keys) * scale, NEGATIVE)
    raised = jnp.exp(scores - jnp.max(scores, axis=1, keepdims=True))
    exact = raised / jnp.sum(raised, axis=1, keepdims=True)
    probs = exact.astype(b16)
    mixed_f[0] = unstack(dot(probs, values)).astype(b16)
    got_mixed = shared_factor(mixed_f)
    got_o.wait_recv()

    def across_rows(at, own, oth):
        sum_send[at, 0] = own.astype(b16)
        sum_send[at, 1] = oth.astype(b16)
        got = copy(sum_send.at[at], sum_recv.at[at], row_peer)
        return got

    own_part, oth_part = dot(mixed_f[0], o_weight[...]), dot(mixed_f[0], o_peer[...])
    got = across_rows(0, own_part, oth_part)
    shared_rest(mixed_f, got_mixed)
    got_down.wait_recv()
    got_col[1].wait_recv()
    grad_activated = dot_back(cot_f[0], down_weight[...]) + dot_back(raw_col[1], down_peer[...])
    got.wait_recv()
    hidden_own = tok_own + (own_part + sum_recv[0, 0].astype(f32))
    hidden_oth = tok_oth + (oth_part + sum_recv[0, 1].astype(f32))

    inverse2 = norm_pair(hidden_own, hidden_oth)
    second_f[0] = (hidden_own * inverse2 * gain2_own).astype(b16)
    second_oth[...] = (hidden_oth * inverse2 * gain2_oth).astype(b16)
    got_second = copy(second_oth, second_f.at[1], col_peer)
    split_factor(second_f)
    got_gate.wait_recv()
    gate_value = dot(second_f[0], gate_weight[...]) + dot(second_oth[...], gate_peer[...])
    got_up.wait_recv()
    up_value = dot(second_f[0], up_weight[...]) + dot(second_oth[...], up_peer[...])
    sigmoid_value = 1.0 / (1.0 + jnp.exp(-gate_value))
    silu_value = gate_value * sigmoid_value
    active_f[0] = (silu_value * up_value).astype(b16)
    grad_gate = (
        grad_activated * up_value * (sigmoid_value * (1.0 + gate_value * (1.0 - sigmoid_value)))
    ).astype(b16)
    grad_up = (grad_activated * silu_value).astype(b16)
    both_f[0, :, :hidden_width] = grad_gate
    both_f[0, :, hidden_width:] = grad_up
    back_own = dot_back(grad_gate, gate_weight[...]) + dot_back(grad_up, up_weight[...])
    back_oth = dot_back(grad_gate, gate_peer[...]) + dot_back(grad_up, up_peer[...])
    got_back = across_rows(1, back_own, back_oth)
    got_both = shared_factor(both_f)
    got_active = shared_factor(active_f)
    split_rest(second_f, got_second)
    out_own, out_oth = dot(active_f[0], down_weight[...]), dot(active_f[0], down_peer[...])
    got_out = across_rows(2, out_own, out_oth)
    got_back.wait_recv()
    back_own = back_own + sum_recv[1, 0].astype(f32)
    back_oth = back_oth + sum_recv[1, 1].astype(f32)

    def norm_back(grad_own, grad_oth, own, oth, inverse, gain_own, gain_oth):
        weighted_own, weighted_oth = grad_own * gain_own, grad_oth * gain_oth
        factor = inverse * inverse * inverse * total(weighted_own * own, weighted_oth * oth) / width
        return (
            weighted_own * inverse - own * factor,
            weighted_oth * inverse - oth * factor,
            jnp.sum(grad_own * own * inverse, axis=0, keepdims=True),
            jnp.sum(grad_oth * oth * inverse, axis=0, keepdims=True),
        )

    hid_own, hid_oth, gain2_part, gain2_rest = norm_back(
        back_own, back_oth, hidden_own, hidden_oth, inverse2, gain2_own, gain2_oth
    )
    hid_own = hid_own + token_own[1].astype(f32)
    hid_oth = hid_oth + raw_col[1].astype(f32)

    branch_f[0] = hid_own.astype(b16)
    branch_oth[...] = hid_oth.astype(b16)
    got_branch = copy(branch_oth, branch_f.at[1], col_peer)
    split_factor(branch_f)
    grad_mixed = (
        dot_back(branch_f[0], o_weight[...]) + dot_back(branch_oth[...], o_peer[...])
    ).astype(b16)
    grad_stack = stack(grad_mixed)
    grad_probs = dot_back(grad_stack, values)
    grad_scores = exact * (grad_probs - jnp.sum(grad_probs * exact, axis=1, keepdims=True))
    grad_scores = grad_scores.astype(b16)
    grad_keys = dot_outer(grad_scores, queries) * scale
    grad_values = dot_outer(probs, grad_stack)
    kv_send[:, :key_width] = grad_keys[rows:].astype(b16)
    kv_send[:, key_width:] = grad_values[rows:].astype(b16)
    got_kv = copy(kv_send, kv_recv, col_peer)
    grad_queries = unstack(dot(grad_scores, keys)) * scale
    split_rest(branch_f, got_branch)
    got_kv.wait_recv()
    grad_keys = grad_keys[:rows] + kv_recv[:, :key_width].astype(f32)
    grad_values = grad_values[:rows] + kv_recv[:, key_width:].astype(f32)
    turn_grad = jnp.concatenate([grad_queries, grad_keys], 1)
    turn_grad = turn_grad * cosine[...] - turned(turn_grad * sine[...])
    projected_f[0] = jnp.concatenate([turn_grad, grad_values], 1).astype(b16)
    part_own = dot_back(projected_f[0], joint[...])
    part_oth = dot_back(projected_f[0], joint_peer[...])
    got_in = across_rows(3, part_own, part_oth)
    got_projected = shared_factor(projected_f)

    got_out.wait_recv()
    out_own = hidden_own + (out_own + sum_recv[2, 0].astype(f32))
    out_oth = hidden_oth + (out_oth + sum_recv[2, 1].astype(f32))
    out_send[0] = out_oth.astype(b16)
    got_output = copy(out_send.at[0], out_recv.at[0], col_peer)
    got_in.wait_recv()
    part_own = part_own + sum_recv[3, 0].astype(f32)
    part_oth = part_oth + sum_recv[3, 1].astype(f32)
    in_own, in_oth, gain1_part, gain1_rest = norm_back(
        part_own, part_oth, tok_own, tok_oth, inverse1, gain1_own, gain1_oth
    )
    in_own = hid_own + in_own
    in_oth = hid_oth + in_oth
    out_send[1] = in_oth.astype(b16)
    got_input = copy(out_send.at[1], out_recv.at[1], col_peer)
    bias_part = jnp.sum(projected_f[0].astype(f32), axis=0, keepdims=True)
    small[...] = jnp.zeros_like(small)
    for at, parts in ((0, (gain1_rest, gain2_rest)), (1, (gain1_part, gain2_part))):
        small[at, 0:1, :half] = parts[0]
        small[at, 1:2, :half] = parts[1]
        small[at, 2:3, :] = bias_part
    got_small = copy(small.at[0], small_got.at[0], col_peer)
    shared_rest(both_f, got_both)
    shared_rest(active_f, got_active)
    shared_rest(projected_f, got_projected)
    got_small.wait_recv()
    small[2] = small[1] + small_got[0]
    got_small = copy(small.at[2], small_got.at[1], x_peer)
    got_output.wait_recv()
    output[...] = jnp.where(diagonal, out_own.astype(b16), out_recv[0])
    got_input.wait_recv()
    input_grad[...] = jnp.where(diagonal, in_own.astype(b16), out_recv[1])
    got_small.wait_recv()
    small_out[...] = small[2] + small_got[1]
    for made in later:
        made.wait_recv()
    for made in started:
        made.wait_send()


def layer_pass(tokens, joint, o_weight, gate_weight, rest):
    rows, half = tokens.shape
    query_width, hidden_width, joint_width = o_weight.shape[0], gate_weight.shape[1], joint.shape[1]
    key_width = (joint_width - query_width) // 2
    b16, f32 = jnp.bfloat16, jnp.float32

    def blocks(width):
        return jax.ShapeDtypeStruct((4, rows, width), b16)

    vmem = pl.BlockSpec(memory_space=pltpu.VMEM)
    outs = [
        jax.ShapeDtypeStruct((rows, half), b16),
        jax.ShapeDtypeStruct((rows, half), b16),
        jax.ShapeDtypeStruct((8, joint_width), f32),
        blocks(half),
        blocks(query_width),
        blocks(half),
        blocks(hidden_width),
        blocks(half),
        blocks(2 * hidden_width),
        blocks(half),
        blocks(joint_width),
    ]
    return pl.pallas_call(
        layer_kernel,
        out_shape=outs,
        in_specs=[vmem] * len(rest),
        out_specs=[vmem] * len(outs),
        scratch_shapes=[
            pltpu.VMEM((half, joint_width), b16),
            pltpu.VMEM((query_width, half), b16),
            pltpu.VMEM((half, hidden_width), b16),
            pltpu.VMEM((half, hidden_width), b16),
            pltpu.VMEM((hidden_width, half), b16),
            pltpu.VMEM((4, 1, half), f32),
            pltpu.VMEM((2, rows, half), b16),
            pltpu.VMEM((2, rows, half), b16),
            pltpu.VMEM((2, rows, half), b16),
            pltpu.VMEM((2, rows, 2 * key_width), b16),
            pltpu.VMEM((rows, half), b16),
            pltpu.VMEM((rows, half), b16),
            pltpu.VMEM((rows, half), b16),
            pltpu.VMEM((4, 2, rows, half), b16),
            pltpu.VMEM((4, 2, rows, half), b16),
            pltpu.VMEM((rows, 2 * key_width), b16),
            pltpu.VMEM((rows, 2 * key_width), b16),
            pltpu.VMEM((2, rows, half), b16),
            pltpu.VMEM((2, rows, half), b16),
            pltpu.VMEM((3, 8, joint_width), f32),
            pltpu.VMEM((2, 8, joint_width), f32),
            pltpu.SemaphoreType.DMA((48,)),
            pltpu.SemaphoreType.DMA((48,)),
        ],
        compiler_params=pltpu.CompilerParams(
            collective_id=1, has_side_effects=True, vmem_limit_bytes=60 * 1024 * 1024
        ),
    )(*rest)


def pair_right(blocks):
    return blocks.reshape(-1, blocks.shape[2])


def per_device(
    tokens,
    seq_lengths,
    cotangent,
    norm1_gain,
    q_weight,
    q_bias,
    k_weight,
    k_bias,
    v_weight,
    v_bias,
    o_weight,
    norm2_gain,
    gate_weight,
    up_weight,
    down_weight,
):
    local_rows = tokens.shape[0]
    group_rows = local_rows * lax.axis_size("row")
    head_rows = group_rows // lax.axis_size("col")
    query_width = q_weight.shape[1]
    key_width = k_weight.shape[1]
    hidden_width = gate_weight.shape[1]
    places, segment, position = sequence_tables(seq_lengths[0], group_rows)
    block_start = lax.axis_index("col") * head_rows

    def from_own(table, how_many):
        return lax.dynamic_slice_in_dim(jnp.concatenate([table, table]), block_start, how_many, 0)

    own_places, own_segment = from_own(places, head_rows), from_own(segment, head_rows)
    key_places, key_segment = from_own(places, group_rows), from_own(segment, group_rows)
    allowed = (own_segment[:, None] == key_segment[None, :]) & (
        key_places[None, :] <= own_places[:, None]
    )
    cosine, sine = rotary_tables(from_own(position, head_rows))
    turn_heads = (query_width + key_width) // HD
    joint_weight = jnp.concatenate([q_weight, k_weight, v_weight], axis=1)
    joint_bias = jnp.concatenate([q_bias, k_bias, v_bias])
    (
        output,
        input_grad,
        small,
        first_f,
        mixed_f,
        second_f,
        active_f,
        cot_f,
        both_f,
        branch_f,
        projected_f,
    ) = layer_pass(
        tokens,
        joint_weight,
        o_weight,
        gate_weight,
        (
            tokens,
            cotangent,
            norm1_gain[None],
            joint_weight,
            joint_bias[None],
            o_weight,
            norm2_gain[None],
            gate_weight,
            up_weight,
            down_weight,
            jnp.tile(cosine, (1, turn_heads)),
            jnp.tile(sine, (1, turn_heads)),
            allowed.astype(jnp.float32),
        ),
    )
    feature_width = tokens.shape[1]
    line = lax.axis_size("dp") // 2
    padding = ((0, 0), (0, 2 * key_width))
    gate_up_total, down_final, joint_total, small_total = line_totals(
        line,
        (
            pair_right(second_f),
            pair_right(both_f),
            pair_right(active_f),
            pair_right(cot_f),
            pair_right(mixed_f),
            jnp.pad(pair_right(branch_f), padding),
            pair_right(first_f),
            pair_right(projected_f),
            small,
        ),
    )
    block = feature_width // (2 * line)
    gate_final, up_final = gate_up_total[:block], gate_up_total[block:]
    output_final, joint_final = joint_total[:block, :query_width], joint_total[block:]
    query_final = joint_final[:, :query_width]
    key_final = joint_final[:, query_width : query_width + key_width]
    value_final = joint_final[:, query_width + key_width :]
    gain1_final, gain2_final = small_total[0, :feature_width], small_total[1, :feature_width]
    qbias_final = small_total[2, :query_width]
    kbias_final = small_total[2, query_width : query_width + key_width]
    vbias_final = small_total[2, query_width + key_width :]
    return (
        output,
        input_grad,
        gain1_final,
        query_final,
        qbias_final,
        key_final,
        kbias_final,
        value_final,
        vbias_final,
        output_final,
        gain2_final,
        gate_final,
        up_final,
        down_final,
    )


def solution(mesh):
    placed = (
        P(("dp", "row"), "col"),
        P("dp", None),
        P(("dp", "row"), "col"),
        P("col"),
        P("col", "row"),
        P("row"),
        P("col", "row"),
        P("row"),
        P("col", "row"),
        P("row"),
        P("row", "col"),
        P("col"),
        P("col", "row"),
        P("col", "row"),
        P("row", "col"),
    )
    return jax.shard_map(
        per_device,
        mesh=mesh,
        in_specs=placed,
        out_specs=(
            P(("dp", "row"), "col"),
            P(("dp", "row"), "col"),
            P("col"),
            P(("col", "dp"), "row"),
            P("row"),
            P(("col", "dp"), "row"),
            P("row"),
            P(("col", "dp"), "row"),
            P("row"),
            P(("row", "dp"), "col"),
            P("col"),
            P(("col", "dp"), "row"),
            P(("col", "dp"), "row"),
            P(("row", "dp"), "col"),
        ),
        check_vma=False,
    )
```
